32 devices in a mesh: groups: 2 (over y), dp: 4 (over z), tensor: 4 (over x, core).
Axes of the slice: x: 2, y: 2, z: 4, core: 2. Of those that a mesh axis runs over, the one named last changes fastest.
Arguments:
- remaining_members: int32 [32], P('groups'), parts along dimension 0, may hold values from 0 to 31, as said below
- allotment: int32 [64], P('groups'), parts along dimension 0, may hold values from 8 to 32
- sample_module_label: int32 [1024], P(('groups', 'dp')), parts along dimension 0, may hold values from 0 to 31, as said below
- block_source_vectors: bfloat16 [1024, 8192], P(('groups', 'dp'), 'tensor'), parts along dimension 0, may hold values from -6 to 6
- fixed_switch_projection: bfloat16 [1024, 28672], P(('groups', 'dp'), 'tensor'), parts along dimension 0, may hold values from -6 to 6
- fixed_expand_projection: bfloat16 [1024, 28672], P(('groups', 'dp'), 'tensor'), parts along dimension 0, may hold values from -6 to 6
- result_adjoint_vectors: bfloat16 [1024, 8192], P(('groups', 'dp'), 'tensor'), parts along dimension 0, may hold values from -6 to 6
- inner_activation_adjoint: bfloat16 [1024, 28672], P(('groups', 'dp'), 'tensor'), parts along dimension 0, may hold values from -6 to 6
- switch_left_matrices: bfloat16 [16384, 256], P(('groups', 'tensor'), 'dp'), parts along dimension 0, may hold values from -0.0625 to 0.0625
- switch_right_matrices: bfloat16 [512, 28672], P(('groups', 'dp'), 'tensor'), parts along dimension 0, may hold values from -0.29882812 to 0.29882812
- expand_left_matrices: bfloat16 [16384, 256], P(('groups', 'tensor'), 'dp'), parts along dimension 0, may hold values from -0.0625 to 0.0625
- expand_right_matrices: bfloat16 [512, 28672], P(('groups', 'dp'), 'tensor'), parts along dimension 0, may hold values from -0.29882812 to 0.29882812
- contract_left_matrices: bfloat16 [57344, 256], P(('groups', 'tensor'), 'dp'), parts along dimension 0, may hold values from -0.03125 to 0.03125
- contract_right_matrices: bfloat16 [512, 8192], P(('groups', 'dp'), 'tensor'), parts along dimension 0, may hold values from -0.29882812 to 0.29882812
Outputs:
- delta_out: bfloat16 [1024, 8192], P(('groups', 'dp'), 'tensor'), parts along dimension 0
- grad_x: bfloat16 [1024, 8192], P(('groups', 'dp'), 'tensor'), parts along dimension 0
- grad_a_gate: float32 [16384, 256], P(('groups', 'tensor'), 'dp'), parts along dimension 0
- gate_output_gradient: float32 [512, 28672], P(('groups', 'dp'), 'tensor'), parts along dimension 0
- grad_a_up: float32 [16384, 256], P(('groups', 'tensor'), 'dp'), parts along dimension 0
- up_output_gradient: float32 [512, 28672], P(('groups', 'dp'), 'tensor'), parts along dimension 0
- grad_a_down: float32 [57344, 256], P(('groups', 'tensor'), 'dp'), parts along dimension 0
- down_output_gradient: float32 [512, 8192], P(('groups', 'dp'), 'tensor'), parts along dimension 0
The draws below stay inside these ranges and needn't reach their ends.
There are 2 independent parts, one for each index of `groups`. The reference program is written for one: setup_inputs(seed, part) draws one part's arguments, and reference() takes and returns one part's arrays. A program takes and returns all parts, laid end to end along the dimension named above; each array names one. Nothing has to cross between parts.
Inputs may be any that keep to these rules, and one draw needn't show every extreme that they name: `remaining_members`: distinct adapter ids. `sample_module_label`: every row names an adapter of the pruning list. Among the rows of one index of dp, the survivors at positions 4 * j to 4 * j + 3 of the list are named at most 32 times together, for every j, and exactly 32 times for some j.
All inputs are finite; a program needn't handle non-finite values.
Results may differ from the reference program's by a relative error of at most 0.0065.
Values may be sent and summed in bfloat16 or wider, within the bound.
A program may use at most 128 MiB of HBM per device.

```python
import jax
import jax.numpy as jnp
from jax import lax

D = 8192
FF = 28672
RANK = 16
SURV_DEV = 4
TOK_DEV = 128
CAP = 32
SURV = 16
ADAPTERS = 32
ROWS = 512
N_DP = 4


def choose_kept_rows(key):
    order = jax.random.permutation(key, ADAPTERS)
    return order[:SURV].astype(jnp.int32)


def draw_remaining_members(key, part):
    return choose_kept_rows(key)


def draw_sample_module_label(key, part):
    picked_rows = choose_kept_rows(key)
    key = jax.random.fold_in(key, 7)
    streams = jax.random.split(key, 3)
    hottest = jax.random.randint(streams[0], (N_DP, 1), 0, max(N_DP // 8, 1))
    placing = jnp.arange(TOK_DEV, dtype=jnp.int32)[None, :]
    spread = (hottest + 1 + jnp.maximum(placing - CAP, 0) % (N_DP - 1)) % N_DP
    destination_device = jnp.where(placing < CAP, hottest, spread)
    device_slot_index = jax.random.randint(streams[1], (N_DP, TOK_DEV), 0, SURV_DEV)
    position = destination_device * SURV_DEV + device_slot_index
    orders = jax.vmap(lambda stream: jax.random.permutation(stream, TOK_DEV))(jax.random.split(streams[2], N_DP))
    position = jnp.take_along_axis(position, orders, axis=1)
    return picked_rows[position.reshape(-1)].astype(jnp.int32)


def place_ends(drawn, own_key, low, top_value):
    dims = drawn.shape
    index_at = [jax.random.randint(jax.random.fold_in(own_key, axis), (), 0, dims[axis]) for axis in range(len(dims))]
    drawn = drawn.at[tuple(index_at)].set(low)
    longest = dims.index(max(dims))
    index_at[longest] = (index_at[longest] + 1) % dims[longest]
    return drawn.at[tuple(index_at)].set(top_value)


def steps_of(rng, dims, cuts, smallest, largest):
    loudness = 1.0
    for dim, parts in cuts:
        draws = jax.random.uniform(jax.random.fold_in(jax.random.fold_in(rng, 6), dim), (parts,), jnp.float32, smallest / len(cuts), largest / len(cuts))
        loudness = loudness * jnp.repeat(jnp.exp(draws), dims[dim] // parts).reshape((-1,) + (1,) * (len(dims) - 1 - dim))
    return loudness


def normal_values(own_key, extent, deviation, bound, cuts=(), held_as=jnp.bfloat16):
    values = deviation * jax.random.normal(own_key, extent, jnp.float32)
    if cuts:
        values = values * steps_of(own_key, extent, cuts, -0.22, 0.18)
    return jnp.clip(values, -bound, bound).astype(held_as)


def setup_inputs(seed: int = 0, part: int = 0) -> dict:
    key_of = jax.random.split(jax.random.key(seed), 15)
    part_splits = jax.random.split(jax.random.fold_in(key_of[14], part), 15)
    return {
        "remaining_members": draw_remaining_members(jax.random.fold_in(jax.random.fold_in(key_of[14], part), 71), part),
        "allotment": place_ends(jax.random.randint(part_splits[1], (ADAPTERS,), 8, 33), jax.random.fold_in(part_splits[1], 1), 8, 32).astype(jnp.int32),
        "sample_module_label": draw_sample_module_label(jax.random.fold_in(jax.random.fold_in(key_of[14], part), 71), part),
        "block_source_vectors": normal_values(part_splits[3], (ROWS, D), 1.0, 6.0, ((0, 4), (1, 4))),
        "fixed_switch_projection": normal_values(part_splits[4], (ROWS, FF), 1.0, 6.0, ((0, 4), (1, 4))),
        "fixed_expand_projection": normal_values(part_splits[5], (ROWS, FF), 1.0, 6.0, ((0, 4), (1, 4))),
        "result_adjoint_vectors": normal_values(part_splits[6], (ROWS, D), 1.0, 6.0, ((0, 4), (1, 4))),
        "inner_activation_adjoint": normal_values(part_splits[7], (ROWS, FF), 1.0, 6.0, ((0, 4), (1, 4))),
        "switch_left_matrices": normal_values(part_splits[8], (D, SURV * RANK), D ** -0.5, 0.0625, ((0, 4), (1, 4))),
        "switch_right_matrices": normal_values(part_splits[9], (SURV * RANK, FF), 0.05, 0.29882812, ((0, 4), (1, 4))),
        "expand_left_matrices": normal_values(part_splits[10], (D, SURV * RANK), D ** -0.5, 0.0625, ((0, 4), (1, 4))),
        "expand_right_matrices": normal_values(part_splits[11], (SURV * RANK, FF), 0.05, 0.29882812, ((0, 4), (1, 4))),
        "contract_left_matrices": normal_values(part_splits[12], (FF, SURV * RANK), FF ** -0.5, 0.03125, ((0, 4), (1, 4))),
        "contract_right_matrices": normal_values(part_splits[13], (SURV * RANK, D), 0.05, 0.29882812, ((0, 4), (1, 4))),
    }


ADAPTER_SCALE = 2.0
WEIGHT_NUM = 16.0


def silu_slope(values):
    logistic = jax.nn.sigmoid(values)
    return logistic * (1.0 + values * (1.0 - logistic))


def reference(remaining_members, allotment, sample_module_label, block_source_vectors, fixed_switch_projection, fixed_expand_projection, result_adjoint_vectors, inner_activation_adjoint, switch_left_matrices, switch_right_matrices, expand_left_matrices, expand_right_matrices, contract_left_matrices, contract_right_matrices):
    entry_places = jnp.arange(SURV, dtype=jnp.int32)
    retained_entry_place = jnp.sum(jnp.where(sample_module_label[:, None] == remaining_members[None, :], entry_places[None, :], 0), axis=1).astype(jnp.int32)
    adapter_ids = jnp.arange(ADAPTERS, dtype=jnp.int32)
    row_quota = jnp.sum(jnp.where(sample_module_label[:, None] == adapter_ids[None, :], allotment[None, :], 0), axis=1)
    token_row_weight = WEIGHT_NUM / row_quota.astype(jnp.float32)
    stack_a_gate = switch_left_matrices.reshape(D, SURV, RANK).transpose(1, 0, 2)
    stack_a_up = expand_left_matrices.reshape(D, SURV, RANK).transpose(1, 0, 2)
    stack_b_gate = switch_right_matrices.reshape(SURV, RANK, FF)
    stack_b_up = expand_right_matrices.reshape(SURV, RANK, FF)
    stack_a_down = contract_left_matrices.reshape(FF, SURV, RANK).transpose(1, 0, 2)
    stack_b_down = contract_right_matrices.reshape(SURV, RANK, D)
    blocks = ROWS // CAP

    def into_device_blocks(array):
        return array.reshape((blocks, CAP) + array.shape[1:])

    def one_block(totals, pieces):
        matrix, gate_preactivation, up_preactivation, cot_outs, cot_hids, owner_position, weight = pieces
        sum_a_gate, gate_output_total, sum_a_up, up_output_total, sum_a_down, down_output_total = totals
        fa_gate = stack_a_gate[owner_position].astype(jnp.float32)
        fa_up = stack_a_up[owner_position].astype(jnp.float32)
        gate_factor_gradient = stack_b_gate[owner_position].astype(jnp.float32)
        up_factor_gradient = stack_b_up[owner_position].astype(jnp.float32)
        fa_down = stack_a_down[owner_position].astype(jnp.float32)
        down_factor_gradient = stack_b_down[owner_position].astype(jnp.float32)
        matrix32 = matrix.astype(jnp.float32)
        gate_rank_rows = jnp.einsum('rd,rdj->rj', matrix32, fa_gate).astype(jnp.bfloat16)
        up_rank_rows = jnp.einsum('rd,rdj->rj', matrix32, fa_up).astype(jnp.bfloat16)
        gate_complete = gate_preactivation.astype(jnp.float32) + ADAPTER_SCALE * jnp.einsum('sh,shw->sw', gate_rank_rows.astype(jnp.float32), gate_factor_gradient)
        up_complete = up_preactivation.astype(jnp.float32) + ADAPTER_SCALE * jnp.einsum('sh,shw->sw', up_rank_rows.astype(jnp.float32), up_factor_gradient)
        activated = gate_complete * jax.nn.sigmoid(gate_complete)
        hidden = (activated * up_complete).astype(jnp.bfloat16)
        hidden32 = hidden.astype(jnp.float32)
        hidden_rank_rows = jnp.einsum('rf,rfj->rj', hidden32, fa_down).astype(jnp.bfloat16)
        adapter_change = (ADAPTER_SCALE * jnp.einsum('tl,tlg->tg', hidden_rank_rows.astype(jnp.float32), down_factor_gradient)).astype(jnp.bfloat16)
        cotangent_scaled_rows = (weight[:, None] * cot_outs.astype(jnp.float32)).astype(jnp.bfloat16)
        hid_scaled = (weight[:, None] * cot_hids.astype(jnp.float32)).astype(jnp.bfloat16)
        cotangent_rank_rows = (ADAPTER_SCALE * jnp.einsum('no,nqo->nq', cotangent_scaled_rows.astype(jnp.float32), down_factor_gradient)).astype(jnp.bfloat16)
        down_output_total = down_output_total.at[owner_position].add(ADAPTER_SCALE * jnp.einsum('mk,ml->mkl', hidden_rank_rows.astype(jnp.float32), cotangent_scaled_rows.astype(jnp.float32)))
        sum_a_down = sum_a_down.at[owner_position].add(jnp.einsum('rf,rj->rfj', hidden32, cotangent_rank_rows.astype(jnp.float32)))
        hidden_grad = hid_scaled.astype(jnp.float32) + jnp.einsum('rj,rfj->rf', cotangent_rank_rows.astype(jnp.float32), fa_down)
        gate_gradient_rows = (hidden_grad * up_complete * silu_slope(gate_complete)).astype(jnp.bfloat16)
        up_gradient_rows = (hidden_grad * activated).astype(jnp.bfloat16)
        gate_backward_pass = (ADAPTER_SCALE * jnp.einsum('le,lve->lv', gate_gradient_rows.astype(jnp.float32), gate_factor_gradient)).astype(jnp.bfloat16)
        up_backward_pass = (ADAPTER_SCALE * jnp.einsum('le,lve->lv', up_gradient_rows.astype(jnp.float32), up_factor_gradient)).astype(jnp.bfloat16)
        gate_output_total = gate_output_total.at[owner_position].add(ADAPTER_SCALE * jnp.einsum('ia,is->ias', gate_rank_rows.astype(jnp.float32), gate_gradient_rows.astype(jnp.float32)))
        up_output_total = up_output_total.at[owner_position].add(ADAPTER_SCALE * jnp.einsum('ia,is->ias', up_rank_rows.astype(jnp.float32), up_gradient_rows.astype(jnp.float32)))
        sum_a_gate = sum_a_gate.at[owner_position].add(jnp.einsum('rd,rj->rdj', matrix32, gate_backward_pass.astype(jnp.float32)))
        sum_a_up = sum_a_up.at[owner_position].add(jnp.einsum('rd,rj->rdj', matrix32, up_backward_pass.astype(jnp.float32)))
        input_grad = jnp.einsum('rj,rdj->rd', gate_backward_pass.astype(jnp.float32), fa_gate) + jnp.einsum('rj,rdj->rd', up_backward_pass.astype(jnp.float32), fa_up)
        totals = (sum_a_gate, gate_output_total, sum_a_up, up_output_total, sum_a_down, down_output_total)
        return totals, (adapter_change, input_grad.astype(jnp.bfloat16))

    start = (jnp.zeros((SURV, D, RANK), jnp.float32), jnp.zeros((SURV, RANK, FF), jnp.float32),
             jnp.zeros((SURV, D, RANK), jnp.float32), jnp.zeros((SURV, RANK, FF), jnp.float32),
             jnp.zeros((SURV, FF, RANK), jnp.float32), jnp.zeros((SURV, RANK, D), jnp.float32))
    inputs = (into_device_blocks(block_source_vectors), into_device_blocks(fixed_switch_projection), into_device_blocks(fixed_expand_projection), into_device_blocks(result_adjoint_vectors),
              into_device_blocks(inner_activation_adjoint), into_device_blocks(retained_entry_place), into_device_blocks(token_row_weight))
    totals, (delta_blocks, grad_blocks) = lax.scan(one_block, start, inputs)
    sum_a_gate, gate_output_total, sum_a_up, up_output_total, sum_a_down, down_output_total = totals
    delta_out = delta_blocks.reshape(ROWS, D)
    grad_x = grad_blocks.reshape(ROWS, D)
    grad_a_gate = sum_a_gate.transpose(1, 0, 2).reshape(D, SURV * RANK)
    grad_a_up = sum_a_up.transpose(1, 0, 2).reshape(D, SURV * RANK)
    grad_a_down = sum_a_down.transpose(1, 0, 2).reshape(FF, SURV * RANK)
    gate_output_gradient = gate_output_total.reshape(SURV * RANK, FF)
    up_output_gradient = up_output_total.reshape(SURV * RANK, FF)
    down_output_gradient = down_output_total.reshape(SURV * RANK, D)
    return (delta_out, grad_x, grad_a_gate, gate_output_gradient, grad_a_up, up_output_gradient, grad_a_down, down_output_gradient)
```

```python
import functools

import jax
import jax.numpy as jnp
from jax import lax
from jax.experimental import pallas as pl
from jax.experimental.pallas import tpu as pltpu
from jax.sharding import PartitionSpec as P

RANK = 16
ADAPTER_SCALE = 2.0
WEIGHT_NUM = 16.0
PARTS = 7
AHEAD = 7
F32 = jnp.float32
BF16 = jnp.bfloat16
MESH = pl.DeviceIdType.MESH


def dot(a, b):
    return jnp.dot(a, b, preferred_element_type=F32)


def dot_nt(a, b):
    return lax.dot_general(a, b, (((1,), (1,)), ((), ())), preferred_element_type=F32)


def iota(shape, axis):
    return lax.broadcasted_iota(jnp.int32, shape, axis)


def one_hot(condition):
    return jnp.where(condition, 1.0, 0.0).astype(BF16)


def kernel(
    sizes,
    label_ref, member_ref, allot_ref,
    x_hbm, gate_hbm, up_hbm, cot_hbm, hid_hbm,
    ag_hbm, bg_hbm, au_hbm, bu_hbm, ad_hbm, bd_hbm,
    delta_hbm, gx_hbm, gag_hbm, gbg_hbm, gau_hbm, gbu_hbm, gad_hbm, gbd_hbm,
    x_in, cot_in, ff_in,
    ag, au, bd, bg, bu, ad,
    x_send, x_recv, cot_send, cot_recv, ff_send, ff_recv,
    low_recv, back_recv, home_send, home_recv,
    gag, gau, gbd, gbg, gbu, gad, delta, gx,
    place, place_t, sg, su, sc,
    in_sem, ffin_sem, out_sem, ffout_sem,
    xs_sem, xr_sem, fs_sem, fr_sem, ts_sem, tr_sem,
):
    dp, nt, cap = sizes
    slots = dp * cap
    rows, width = x_in.shape
    part = ff_in.shape[2] // 3
    ranks = ag.shape[0]
    kept = ranks // RANK
    sub = 256 if part % 256 == 0 else part
    me = lax.axis_index("dp")
    tme = lax.axis_index("tensor")
    barrier = pltpu.get_barrier_semaphore()
    for d in range(1, dp):
        pl.semaphore_signal(barrier, inc=1, device_id={"dp": lax.rem(me + d, dp)}, device_id_type=MESH)
    for d in range(1, nt):
        pl.semaphore_signal(barrier, inc=1, device_id={"tensor": lax.rem(tme + d, nt)}, device_id_type=MESH)

    first = [
        pltpu.make_async_copy(source, target, in_sem.at[n])
        for n, (source, target) in enumerate((
            (x_hbm, x_in), (cot_hbm, cot_in), (ag_hbm, ag), (au_hbm, au), (bd_hbm, bd),
            (bg_hbm, bg), (bu_hbm, bu), (ad_hbm, ad),
        ))
    ]

    def ff_load(k):
        at = pl.ds(pl.multiple_of(k * part, 128), part)
        return [
            pltpu.make_async_copy(
                source.at[:, at], ff_in.at[k, :, pl.ds(n * part, part)], ffin_sem.at[n, k]
            )
            for n, source in enumerate((gate_hbm, up_hbm, hid_hbm))
        ]

    first[0].start()
    first[1].start()

    @pl.loop(0, PARTS)
    def _(k):
        for copy in ff_load(k):
            copy.start()

    for copy in first[2:]:
        copy.start()

    label_col = jnp.transpose(jnp.broadcast_to(label_ref[...].astype(F32), (128, rows)))[:, :1]
    members = member_ref[...].astype(F32)
    n_surv = members.shape[1]
    pos_col = jnp.sum(
        jnp.where(label_col == members, iota((rows, n_surv), 1).astype(F32), 0.0), axis=1, keepdims=True
    )
    n_adapt = allot_ref.shape[1]
    quota = jnp.sum(
        jnp.where(label_col == iota((rows, n_adapt), 1).astype(F32), allot_ref[...].astype(F32), 0.0),
        axis=1, keepdims=True,
    )
    weight = WEIGHT_NUM / quota
    pos = jnp.transpose(jnp.broadcast_to(pos_col, (rows, 128)))[:8].astype(jnp.int32)[:1]
    wide = max(8, -(-dp // 8) * 8)
    dest_ids = iota((wide, rows), 0)
    chosen = (pos >= dest_ids * kept) & (pos < dest_ids * kept + kept)
    chosen_f = jnp.where(chosen, 1.0, 0.0)
    before = one_hot(iota((rows, rows), 0) < iota((rows, rows), 1))
    earlier = dot(chosen_f.astype(BF16), before)
    dest = jnp.sum(jnp.where(chosen, dest_ids.astype(F32), 0.0), axis=0, keepdims=True)
    rank = jnp.sum(chosen_f * earlier, axis=0, keepdims=True)
    placing = (dest * cap + rank).astype(jnp.int32)
    hot = jnp.where(iota((slots, rows), 0) == placing, 1.0, 0.0)
    place[...] = hot.astype(BF16)
    place_t[...] = jnp.transpose(hot).astype(BF16)
    own = pos - (dest * kept).astype(jnp.int32)
    lanes = iota((128, rows), 0)
    mask_home = one_hot((lanes >= own * RANK) & (lanes < own * RANK + RANK))

    def peer_copy(d, source, target, send_sem, recv_sem):
        peer = lax.rem(me + d, dp)
        return pltpu.make_async_remote_copy(
            src_ref=source(peer), dst_ref=target(me), send_sem=send_sem, recv_sem=recv_sem,
            device_id={"dp": peer}, device_id_type=MESH,
        )

    def x_copy(d):
        return peer_copy(d, lambda p: x_send.at[p], lambda p: x_recv.at[p], xs_sem.at[0, d], xr_sem.at[0, d])

    def cot_copy(d):
        return peer_copy(d, lambda p: cot_send.at[p], lambda p: cot_recv.at[p], xs_sem.at[1, d], xr_sem.at[1, d])

    def home_copy(d):
        return peer_copy(d, lambda p: home_send.at[p], lambda p: home_recv.at[p], xs_sem.at[2, d], xr_sem.at[2, d])

    def ff_copy(k, d):
        return peer_copy(
            d, lambda p: ff_send.at[k, p], lambda p: ff_recv.at[k, p], fs_sem.at[k, d], fr_sem.at[k, d]
        )

    def tensor_copy(which, buffer, d):
        peer = lax.rem(tme + d, nt)
        return pltpu.make_async_remote_copy(
            src_ref=buffer.at[tme], dst_ref=buffer.at[tme], send_sem=ts_sem.at[which, d],
            recv_sem=tr_sem.at[which, d], device_id={"tensor": peer}, device_id_type=MESH,
        )

    def by_device(values):
        return values.astype(BF16).reshape(dp, cap, values.shape[1])

    hot_rows = place[...]
    first[0].wait()
    x_send[:, :, 0:128] = by_device(dot_nt(hot_rows, mask_home))
    x_send[:, :, 128:] = by_device(dot(hot_rows, x_in[...]))
    pl.semaphore_wait(barrier, dp - 1 + nt - 1)
    for d in range(1, dp):
        x_copy(d).start()
    x_recv[me] = x_send[me]
    first[1].wait()
    cot_send[...] = by_device(dot(hot_rows, (weight * cot_in[...].astype(F32)).astype(BF16)))
    for d in range(1, dp):
        cot_copy(d).start()
    cot_recv[me] = cot_send[me]

    def send_part(k):
        for copy in ff_load(k):
            copy.wait()
        hot_now = place[...]
        for n in range(3):
            piece = ff_in[k, :, n * part:(n + 1) * part]
            if n == 2:
                piece = (weight * piece.astype(F32)).astype(BF16)
            ff_send[k, :, :, n * part:(n + 1) * part] = by_device(dot(hot_now, piece))
        for d in range(1, dp):
            ff_copy(k, d).start()
        ff_recv[k, me] = ff_send[k, me]

    @pl.loop(0, min(AHEAD, PARTS))
    def _(k):
        send_part(k)

    for copy in first[2:]:
        copy.wait()
    for d in range(1, dp):
        x_copy(d).wait_recv()
    mask = jnp.transpose(x_recv[:, :, 0:128].reshape(slots, 128).astype(F32))[:ranks]

    def select(values):
        masked = values * mask
        total = masked[0:RANK]
        for n in range(1, kept):
            total = total + masked[n * RANK:(n + 1) * RANK]
        return total

    def spread(values):
        return jnp.concatenate([values] * kept, axis=0) * mask

    x_rows = x_recv[:, :, 128:].reshape(slots, width)
    low_recv[tme, 0:RANK] = select(dot_nt(ag[...], x_rows))
    low_recv[tme, RANK:2 * RANK] = select(dot_nt(au[...], x_rows))
    for d in range(1, dp):
        cot_copy(d).wait_recv()
    low_recv[tme, 2 * RANK:] = select(dot_nt(bd[...], cot_recv[...].reshape(slots, width)))
    for d in range(1, nt):
        tensor_copy(0, low_recv, d).start()
    for d in range(1, nt):
        tensor_copy(0, low_recv, d).wait_recv()
    low = jnp.sum(low_recv[...], axis=0)
    sg_t = spread(low[0:RANK].astype(BF16).astype(F32))
    su_t = spread(low[RANK:2 * RANK].astype(BF16).astype(F32))
    sc_t = spread((ADAPTER_SCALE * low[2 * RANK:]).astype(BF16).astype(F32))
    sg[...] = jnp.transpose(sg_t).astype(BF16)
    su[...] = jnp.transpose(su_t).astype(BF16)
    sc[...] = jnp.transpose(sc_t).astype(BF16)
    sg_t, su_t, sc_t = sg_t.astype(BF16), su_t.astype(BF16), sc_t.astype(BF16)

    def ff_store(k):
        at = pl.ds(pl.multiple_of(k * part, 128), part)
        return [
            pltpu.make_async_copy(source.at[:, at], target.at[:, at], ffout_sem.at[n, k])
            for n, (source, target) in enumerate(((gbg, gbg_hbm), (gbu, gbu_hbm), (gad, gad_hbm)))
        ]

    def ff_part(k, totals):
        for d in range(1, dp):
            ff_copy(k, d).wait_recv()

        def ff_sub(j, totals):
            low_h, back_g, back_u = totals
            at = pl.ds(pl.multiple_of(k * part + j * sub, 128), sub)

            def piece(n):
                start = pl.multiple_of(n * part + j * sub, 128)
                return ff_recv[k, :, :, pl.ds(start, sub)].reshape(slots, sub).astype(F32)

            bg_now, bu_now, ad_now = bg[:, at], bu[:, at], ad[:, at]
            gate_full = piece(0) + ADAPTER_SCALE * dot(sg[...], bg_now)
            up_full = piece(1) + ADAPTER_SCALE * dot(su[...], bu_now)
            logistic = jax.nn.sigmoid(gate_full)
            activated = gate_full * logistic
            hidden = (activated * up_full).astype(BF16)
            hidden_grad = piece(2) + dot(sc[...], ad_now)
            slope = logistic * (1.0 + gate_full * (1.0 - logistic))
            gate_grad = (hidden_grad * up_full * slope).astype(BF16)
            up_grad = (hidden_grad * activated).astype(BF16)
            gbg[:, at] = ADAPTER_SCALE * dot(sg_t, gate_grad)
            gbu[:, at] = ADAPTER_SCALE * dot(su_t, up_grad)
            gad[:, at] = dot(sc_t, hidden)
            return (
                low_h + dot_nt(ad_now, hidden),
                back_g + dot_nt(bg_now, gate_grad),
                back_u + dot_nt(bu_now, up_grad),
            )

        totals = lax.fori_loop(0, part // sub, ff_sub, totals)
        for copy in ff_store(k):
            copy.start()
        if AHEAD < PARTS:
            @pl.when(k + AHEAD < PARTS)
            def _():
                send_part(k + AHEAD)
        return totals

    zero = jnp.zeros((ranks, slots), F32)
    low_h, back_g, back_u = lax.fori_loop(0, PARTS, ff_part, (zero, zero, zero))
    back_recv[tme, 0:RANK] = select(low_h)
    back_recv[tme, RANK:2 * RANK] = select(back_g)
    back_recv[tme, 2 * RANK:] = select(back_u)
    for d in range(1, nt):
        tensor_copy(1, back_recv, d).start()
    for d in range(1, nt):
        tensor_copy(1, back_recv, d).wait_recv()
    back = jnp.sum(back_recv[...], axis=0)
    sh_t = spread(back[0:RANK].astype(BF16).astype(F32))
    sbg_t = spread((ADAPTER_SCALE * back[RANK:2 * RANK]).astype(BF16).astype(F32))
    sbu_t = spread((ADAPTER_SCALE * back[2 * RANK:]).astype(BF16).astype(F32))
    sh = jnp.transpose(sh_t).astype(BF16)
    sbg = jnp.transpose(sbg_t).astype(BF16)
    sbu = jnp.transpose(sbu_t).astype(BF16)
    home_send[:, :, 0:width] = by_device(ADAPTER_SCALE * dot(sh, bd[...]))
    home_send[:, :, width:] = by_device(dot(sbg, ag[...]) + dot(sbu, au[...]))
    for d in range(1, dp):
        home_copy(d).start()
    home_recv[me] = home_send[me]
    gbd[...] = ADAPTER_SCALE * dot(sh_t.astype(BF16), cot_recv[...].reshape(slots, width))
    x_rows = x_recv[:, :, 128:].reshape(slots, width)
    gag[...] = dot(sbg_t.astype(BF16), x_rows)
    gau[...] = dot(sbu_t.astype(BF16), x_rows)
    last = [
        pltpu.make_async_copy(source, target, out_sem.at[n])
        for n, (source, target) in enumerate((
            (gbd, gbd_hbm), (gag, gag_hbm), (gau, gau_hbm), (delta, delta_hbm), (gx, gx_hbm)
        ))
    ]
    for copy in last[:3]:
        copy.start()
    for d in range(1, dp):
        home_copy(d).wait_recv()
    back_rows = place_t[...]
    delta[...] = dot(back_rows, home_recv[:, :, 0:width].reshape(slots, width)).astype(BF16)
    last[3].start()
    gx[...] = dot(back_rows, home_recv[:, :, width:].reshape(slots, width)).astype(BF16)
    last[4].start()

    for d in range(1, dp):
        x_copy(d).wait_send()
        cot_copy(d).wait_send()
        home_copy(d).wait_send()
    for d in range(1, nt):
        tensor_copy(0, low_recv, d).wait_send()
        tensor_copy(1, back_recv, d).wait_send()

    @pl.loop(0, PARTS)
    def _(k):
        for d in range(1, dp):
            ff_copy(k, d).wait_send()
        for copy in ff_store(k):
            copy.wait()

    for copy in last:
        copy.wait()


def on_device(
    remaining_members, allotment, sample_module_label, block_source_vectors,
    fixed_switch_projection, fixed_expand_projection, result_adjoint_vectors,
    inner_activation_adjoint, switch_left_matrices, switch_right_matrices,
    expand_left_matrices, expand_right_matrices, contract_left_matrices, contract_right_matrices,
):
    dp, nt = lax.axis_size("dp"), lax.axis_size("tensor")
    rows, width = block_source_vectors.shape
    hidden_units = fixed_switch_projection.shape[1]
    ranks = switch_right_matrices.shape[0]
    cap = max(rows // 8, rows // dp)
    slots = dp * cap
    part = hidden_units // PARTS

    def f32(*shape):
        return jax.ShapeDtypeStruct(shape, F32)

    anywhere = pl.BlockSpec(memory_space=pl.ANY)
    whole = pl.BlockSpec(memory_space=pltpu.VMEM)
    dma = pltpu.SemaphoreType.DMA
    outs = pl.pallas_call(
        functools.partial(kernel, (dp, nt, cap)),
        out_shape=(
            jax.ShapeDtypeStruct((rows, width), BF16),
            jax.ShapeDtypeStruct((rows, width), BF16),
            f32(ranks, width), f32(ranks, hidden_units),
            f32(ranks, width), f32(ranks, hidden_units),
            f32(ranks, hidden_units), f32(ranks, width),
        ),
        in_specs=[whole] * 3 + [anywhere] * 11,
        out_specs=[anywhere] * 8,
        scratch_shapes=[
            pltpu.VMEM((rows, width), BF16), pltpu.VMEM((rows, width), BF16),
            pltpu.VMEM((PARTS, rows, 3 * part), BF16),
            pltpu.VMEM((ranks, width), BF16), pltpu.VMEM((ranks, width), BF16),
            pltpu.VMEM((ranks, width), BF16),
            pltpu.VMEM((ranks, hidden_units), BF16), pltpu.VMEM((ranks, hidden_units), BF16),
            pltpu.VMEM((ranks, hidden_units), BF16),
            pltpu.VMEM((dp, cap, 128 + width), BF16), pltpu.VMEM((dp, cap, 128 + width), BF16),
            pltpu.VMEM((dp, cap, width), BF16), pltpu.VMEM((dp, cap, width), BF16),
            pltpu.VMEM((PARTS, dp, cap, 3 * part), BF16), pltpu.VMEM((PARTS, dp, cap, 3 * part), BF16),
            pltpu.VMEM((nt, 3 * RANK, slots), F32), pltpu.VMEM((nt, 3 * RANK, slots), F32),
            pltpu.VMEM((dp, cap, 2 * width), BF16), pltpu.VMEM((dp, cap, 2 * width), BF16),
            pltpu.VMEM((ranks, width), F32), pltpu.VMEM((ranks, width), F32),
            pltpu.VMEM((ranks, width), F32),
            pltpu.VMEM((ranks, hidden_units), F32), pltpu.VMEM((ranks, hidden_units), F32),
            pltpu.VMEM((ranks, hidden_units), F32),
            pltpu.VMEM((rows, width), BF16), pltpu.VMEM((rows, width), BF16),
            pltpu.VMEM((slots, rows), BF16), pltpu.VMEM((rows, slots), BF16),
            pltpu.VMEM((slots, ranks), BF16), pltpu.VMEM((slots, ranks), BF16),
            pltpu.VMEM((slots, ranks), BF16),
            dma((8,)), dma((3, PARTS)), dma((5,)), dma((3, PARTS)),
            dma((3, dp)), dma((3, dp)), dma((PARTS, dp)), dma((PARTS, dp)),
            dma((2, nt)), dma((2, nt)),
        ],
        compiler_params=pltpu.CompilerParams(
            collective_id=0, has_side_effects=True, vmem_limit_bytes=56 * 2**20
        ),
        cost_estimate=pl.CostEstimate(flops=3 * 10**9, bytes_accessed=20 * 2**20, transcendentals=10**6),
    )(
        sample_module_label.reshape(1, -1), remaining_members.reshape(1, -1), allotment.reshape(1, -1),
        block_source_vectors, fixed_switch_projection, fixed_expand_projection,
        result_adjoint_vectors, inner_activation_adjoint,
        switch_left_matrices.T, switch_right_matrices, expand_left_matrices.T,
        expand_right_matrices, contract_left_matrices.T, contract_right_matrices,
    )
    delta, gx, gag, gbg, gau, gbu, gad, gbd = outs
    return delta, gx, gag.T, gbg, gau.T, gbu, gad.T, gbd


def solution(mesh):
    rows = P(("groups", "dp"), "tensor")
    left = P(("groups", "tensor"), "dp")
    in_specs = (
        P("groups"), P("groups"), P(("groups", "dp")),
        rows, rows, rows, rows, rows,
        left, rows, left, rows, left, rows,
    )
    out_specs = (rows, rows, left, rows, left, rows, left, rows)
    return jax.shard_map(
        on_device, mesh=mesh, in_specs=in_specs, out_specs=out_specs, check_vma=False
    )
```

```python
import functools

import jax
import jax.numpy as jnp
from jax import lax
from jax.experimental import pallas as pl
from jax.experimental.pallas import tpu as pltpu
from jax.sharding import PartitionSpec as P

RANK = 16
ADAPTER_SCALE = 2.0
WEIGHT_NUM = 16.0
PARTS = 7
F32 = jnp.float32
BF16 = jnp.bfloat16
MESH = pl.DeviceIdType.MESH


def dot(a, b):
    return jnp.dot(a, b, preferred_element_type=F32)


def dot_nt(a, b):
    return lax.dot_general(a, b, (((1,), (1,)), ((), ())), preferred_element_type=F32)


def iota(shape, axis):
    return lax.broadcasted_iota(jnp.int32, shape, axis)


def one_hot(condition):
    return jnp.where(condition, 1.0, 0.0).astype(BF16)


def kernel(
    sizes,
    label_hbm, member_hbm, allot_hbm,
    x_hbm, gate_hbm, up_hbm, cot_hbm, hid_hbm,
    ag_hbm, bg_hbm, au_hbm, bu_hbm, ad_hbm, bd_hbm,
    delta, gx, gag, gbg, gau, gbu, gad, gbd,
    label_ref, member_ref, allot_ref, x_in, cot_in, gu_in, hid_in,
    ag, au, bd, bg, bu, ad,
    x_send, x_recv, cot_send, cot_recv, gu_send, gu_recv, hid_send, hid_recv,
    low_recv, cot_sums, hidden_sums, back_recv,
    delta_send, delta_recv, gx_send, gx_recv, up_slope, acted,
    hiddens, place, place_t, sg, su, sc,
    in_sem, ffin_sem,
    xs_sem, xr_sem, fs_sem, fr_sem, ts_sem, tr_sem,
):
    dp, nt, cap = sizes
    slots = dp * cap
    rows, width = x_in.shape
    part = hid_in.shape[2]
    ranks = ag.shape[0]
    kept = ranks // RANK
    sub = 256 if part % 256 == 0 else part
    me = lax.axis_index("dp")
    tme = lax.axis_index("tensor")
    barrier = pltpu.get_barrier_semaphore()
    for d in range(1, dp):
        pl.semaphore_signal(barrier, inc=1, device_id={"dp": lax.rem(me + d, dp)}, device_id_type=MESH)
    for d in range(1, nt):
        pl.semaphore_signal(barrier, inc=1, device_id={"tensor": lax.rem(tme + d, nt)}, device_id_type=MESH)

    first = [
        pltpu.make_async_copy(source, target, in_sem.at[n])
        for n, (source, target) in enumerate((
            (x_hbm, x_in), (cot_hbm, cot_in), (ag_hbm, ag), (au_hbm, au), (bd_hbm, bd),
            (bg_hbm, bg), (bu_hbm, bu), (ad_hbm, ad),
        ))
    ]
    plan = [
        pltpu.make_async_copy(source, target, in_sem.at[8 + n])
        for n, (source, target) in enumerate((
            (label_hbm, label_ref), (member_hbm, member_ref), (allot_hbm, allot_ref),
        ))
    ]
    for copy in plan:
        copy.start()

    def gu_load(k):
        at = pl.ds(pl.multiple_of(k * part, 128), part)
        return [
            pltpu.make_async_copy(
                source.at[:, at], gu_in.at[k, :, pl.ds(n * part, part)], ffin_sem.at[n, k]
            )
            for n, source in enumerate((gate_hbm, up_hbm))
        ]

    def hid_load(k):
        at = pl.ds(pl.multiple_of(k * part, 128), part)
        return pltpu.make_async_copy(hid_hbm.at[:, at], hid_in.at[k], ffin_sem.at[2, k])

    first[0].start()

    @pl.loop(0, PARTS)
    def _(k):
        for copy in gu_load(k):
            copy.start()

    first[1].start()

    @pl.loop(0, PARTS)
    def _(k):
        hid_load(k).start()

    for copy in first[2:]:
        copy.start()

    for copy in plan:
        copy.wait()
    label_col = jnp.transpose(jnp.broadcast_to(label_ref[...].astype(F32), (128, rows)))[:, :1]
    members = member_ref[...].astype(F32)
    n_surv = members.shape[1]
    pos_col = jnp.sum(
        jnp.where(label_col == members, iota((rows, n_surv), 1).astype(F32), 0.0), axis=1, keepdims=True
    )
    n_adapt = allot_ref.shape[1]
    quota = jnp.sum(
        jnp.where(label_col == iota((rows, n_adapt), 1).astype(F32), allot_ref[...].astype(F32), 0.0),
        axis=1, keepdims=True,
    )
    weight = WEIGHT_NUM / quota
    pos = jnp.transpose(jnp.broadcast_to(pos_col, (rows, 128)))[:8].astype(jnp.int32)[:1]
    wide = max(8, -(-dp // 8) * 8)
    dest_ids = iota((wide, rows), 0)
    chosen = (pos >= dest_ids * kept) & (pos < dest_ids * kept + kept)
    chosen_f = jnp.where(chosen, 1.0, 0.0)
    before = one_hot(iota((rows, rows), 0) < iota((rows, rows), 1))
    earlier = dot(chosen_f.astype(BF16), before)
    dest = jnp.sum(jnp.where(chosen, dest_ids.astype(F32), 0.0), axis=0, keepdims=True)
    rank = jnp.sum(chosen_f * earlier, axis=0, keepdims=True)
    placing = (dest * cap + rank).astype(jnp.int32)
    hot = jnp.where(iota((slots, rows), 0) == placing, 1.0, 0.0)
    place[...] = hot.astype(BF16)
    place_t[...] = jnp.transpose(hot).astype(BF16)
    own = pos - (dest * kept).astype(jnp.int32)
    lanes = iota((128, rows), 0)
    mask_home = one_hot((lanes >= own * RANK) & (lanes < own * RANK + RANK))

    def peer_copy(d, source, target, send_sem, recv_sem):
        peer = lax.rem(me + d, dp)
        return pltpu.make_async_remote_copy(
            src_ref=source(peer), dst_ref=target(me), send_sem=send_sem, recv_sem=recv_sem,
            device_id={"dp": peer}, device_id_type=MESH,
        )

    def x_copy(d):
        return peer_copy(d, lambda p: x_send.at[p], lambda p: x_recv.at[p], xs_sem.at[0, d], xr_sem.at[0, d])

    def cot_copy(d):
        return peer_copy(d, lambda p: cot_send.at[p], lambda p: cot_recv.at[p], xs_sem.at[1, d], xr_sem.at[1, d])

    def delta_copy(d):
        return peer_copy(d, lambda p: delta_send.at[p], lambda p: delta_recv.at[p], xs_sem.at[2, d], xr_sem.at[2, d])

    def gx_copy(d):
        return peer_copy(d, lambda p: gx_send.at[p], lambda p: gx_recv.at[p], xs_sem.at[3, d], xr_sem.at[3, d])

    def gu_copy(k, d):
        return peer_copy(
            d, lambda p: gu_send.at[k, p], lambda p: gu_recv.at[k, p], fs_sem.at[0, k, d], fr_sem.at[0, k, d]
        )

    def hid_copy(k, d):
        return peer_copy(
            d, lambda p: hid_send.at[k, p], lambda p: hid_recv.at[k, p], fs_sem.at[1, k, d], fr_sem.at[1, k, d]
        )

    def tensor_copy(which, buffer, d):
        peer = lax.rem(tme + d, nt)
        return pltpu.make_async_remote_copy(
            src_ref=buffer.at[tme], dst_ref=buffer.at[tme], send_sem=ts_sem.at[which, d],
            recv_sem=tr_sem.at[which, d], device_id={"tensor": peer}, device_id_type=MESH,
        )

    def by_device(values):
        return values.astype(BF16).reshape(dp, cap, values.shape[1])

    hot_rows = place[...]
    first[0].wait()
    x_send[:, :, 0:128] = by_device(dot_nt(hot_rows, mask_home))
    x_send[:, :, 128:] = by_device(dot(hot_rows, x_in[...]))
    pl.semaphore_wait(barrier, dp - 1 + nt - 1)
    for d in range(1, dp):
        x_copy(d).start()
    x_recv[me] = x_send[me]

    @pl.loop(0, PARTS)
    def _(k):
        for copy in gu_load(k):
            copy.wait()
        gu_send[k] = by_device(dot(place[...], gu_in[k]))
        for d in range(1, dp):
            gu_copy(k, d).start()
        gu_recv[k, me] = gu_send[k, me]

    first[1].wait()
    cot_send[...] = by_device(dot(hot_rows, (weight * cot_in[...].astype(F32)).astype(BF16)))
    for d in range(1, dp):
        cot_copy(d).start()
    cot_recv[me] = cot_send[me]

    @pl.loop(0, PARTS)
    def _(k):
        hid_load(k).wait()
        hid_send[k] = by_device(dot(place[...], (weight * hid_in[k].astype(F32)).astype(BF16)))
        for d in range(1, dp):
            hid_copy(k, d).start()
        hid_recv[k, me] = hid_send[k, me]

    for copy in first[2:]:
        copy.wait()
    for d in range(1, dp):
        x_copy(d).wait_recv()
    mask = jnp.transpose(x_recv[:, :, 0:128].reshape(slots, 128).astype(F32))[:ranks]

    def select(values):
        masked = values * mask
        total = masked[0:RANK]
        for n in range(1, kept):
            total = total + masked[n * RANK:(n + 1) * RANK]
        return total

    def spread(values):
        return jnp.concatenate([values] * kept, axis=0) * mask

    x_rows = x_recv[:, :, 128:].reshape(slots, width)
    low_recv[tme, 0:RANK] = select(dot_nt(ag[...], x_rows))
    low_recv[tme, RANK:2 * RANK] = select(dot_nt(au[...], x_rows))
    def exchange(which, buffer):
        for d in range(1, nt):
            tensor_copy(which, buffer, d).start()
        for d in range(1, nt):
            tensor_copy(which, buffer, d).wait_recv()
        return jnp.sum(buffer[...], axis=0)

    low = exchange(0, low_recv)
    sg_t = spread(low[0:RANK].astype(BF16).astype(F32))
    su_t = spread(low[RANK:].astype(BF16).astype(F32))
    sg[...] = jnp.transpose(sg_t).astype(BF16)
    su[...] = jnp.transpose(su_t).astype(BF16)

    def columns(k, j):
        return pl.ds(pl.multiple_of(k * part + j * sub, 128), sub)

    def forward(k, total):
        for d in range(1, dp):
            gu_copy(k, d).wait_recv()

        def forward_sub(j, total):
            at = columns(k, j)

            def piece(n):
                start = pl.multiple_of(n * part + j * sub, 128)
                return gu_recv[k, :, :, pl.ds(start, sub)].reshape(slots, sub).astype(F32)

            gate_full = piece(0) + ADAPTER_SCALE * dot(sg[...], bg[:, at])
            up_full = piece(1) + ADAPTER_SCALE * dot(su[...], bu[:, at])
            logistic = jax.nn.sigmoid(gate_full)
            activated = gate_full * logistic
            hidden = (activated * up_full).astype(BF16)
            acted[:, at] = activated
            up_slope[:, at] = up_full * (logistic * (1.0 + gate_full * (1.0 - logistic)))
            hiddens[:, at] = hidden
            return total + dot_nt(ad[:, at], hidden)

        return lax.fori_loop(0, part // sub, forward_sub, total)

    zero = jnp.zeros((ranks, slots), F32)
    hidden_sums[tme] = select(lax.fori_loop(0, PARTS, forward, zero))
    sh_t = spread(exchange(1, hidden_sums).astype(BF16).astype(F32))
    delta_send[...] = by_device(ADAPTER_SCALE * dot(jnp.transpose(sh_t).astype(BF16), bd[...]))
    for d in range(1, dp):
        delta_copy(d).start()
    delta_recv[me] = delta_send[me]

    for d in range(1, dp):
        cot_copy(d).wait_recv()
    cot_rows = cot_recv[...].reshape(slots, width)
    cot_sums[tme] = select(dot_nt(bd[...], cot_rows))
    sc_t = spread((ADAPTER_SCALE * exchange(2, cot_sums)).astype(BF16).astype(F32))
    sc[...] = jnp.transpose(sc_t).astype(BF16)
    gbd[...] = ADAPTER_SCALE * dot(sh_t.astype(BF16), cot_rows)
    sg_t, su_t, sc_t = sg_t.astype(BF16), su_t.astype(BF16), sc_t.astype(BF16)

    def backward(k, totals):
        for d in range(1, dp):
            hid_copy(k, d).wait_recv()

        def backward_sub(j, totals):
            back_g, back_u = totals
            at = columns(k, j)
            arrived = hid_recv[k, :, :, pl.ds(pl.multiple_of(j * sub, 128), sub)].reshape(slots, sub)
            hidden_grad = arrived.astype(F32) + dot(sc[...], ad[:, at])
            gate_grad = (hidden_grad * up_slope[:, at]).astype(BF16)
            up_grad = (hidden_grad * acted[:, at]).astype(BF16)
            gbg[:, at] = ADAPTER_SCALE * dot(sg_t, gate_grad)
            gbu[:, at] = ADAPTER_SCALE * dot(su_t, up_grad)
            gad[:, at] = dot(sc_t, hiddens[:, at])
            return back_g + dot_nt(bg[:, at], gate_grad), back_u + dot_nt(bu[:, at], up_grad)

        return lax.fori_loop(0, part // sub, backward_sub, totals)

    back_g, back_u = lax.fori_loop(0, PARTS, backward, (zero, zero))
    back_recv[tme, 0:RANK] = select(back_g)
    back_recv[tme, RANK:] = select(back_u)
    back = ADAPTER_SCALE * exchange(3, back_recv)
    sbg_t = spread(back[0:RANK].astype(BF16).astype(F32))
    sbu_t = spread(back[RANK:].astype(BF16).astype(F32))
    sbg = jnp.transpose(sbg_t).astype(BF16)
    sbu = jnp.transpose(sbu_t).astype(BF16)
    gx_send[...] = by_device(dot(sbg, ag[...]) + dot(sbu, au[...]))
    for d in range(1, dp):
        gx_copy(d).start()
    gx_recv[me] = gx_send[me]
    x_rows = x_recv[:, :, 128:].reshape(slots, width)
    gag[...] = dot(sbg_t.astype(BF16), x_rows)
    gau[...] = dot(sbu_t.astype(BF16), x_rows)
    for d in range(1, dp):
        delta_copy(d).wait_recv()
    delta[...] = dot(place_t[...], delta_recv[...].reshape(slots, width)).astype(BF16)
    for d in range(1, dp):
        x_copy(d).wait_send()
        cot_copy(d).wait_send()
        delta_copy(d).wait_send()
    for n, buffer in enumerate((low_recv, hidden_sums, cot_sums, back_recv)):
        for d in range(1, nt):
            tensor_copy(n, buffer, d).wait_send()

    @pl.loop(0, PARTS)
    def _(k):
        for d in range(1, dp):
            gu_copy(k, d).wait_send()
            hid_copy(k, d).wait_send()

    for d in range(1, dp):
        gx_copy(d).wait_recv()
    gx[...] = dot(place_t[...], gx_recv[...].reshape(slots, width)).astype(BF16)
    for d in range(1, dp):
        gx_copy(d).wait_send()


def write_out(*refs):
    n = len(refs) // 2
    sems = refs[-1]
    copies = [pltpu.make_async_copy(refs[i], refs[n + i], sems.at[i]) for i in range(n)]
    for copy in copies:
        copy.start()
    for copy in copies:
        copy.wait()


def on_device(
    remaining_members, allotment, sample_module_label, block_source_vectors,
    fixed_switch_projection, fixed_expand_projection, result_adjoint_vectors,
    inner_activation_adjoint, switch_left_matrices, switch_right_matrices,
    expand_left_matrices, expand_right_matrices, contract_left_matrices, contract_right_matrices,
):
    dp, nt = lax.axis_size("dp"), lax.axis_size("tensor")
    rows, width = block_source_vectors.shape
    hidden_units = fixed_switch_projection.shape[1]
    ranks = switch_right_matrices.shape[0]
    cap = max(rows // 8, rows // dp)
    slots = dp * cap
    part = hidden_units // PARTS

    out_forms = [
        ((rows, width), BF16), ((rows, width), BF16),
        ((ranks, width), F32), ((ranks, hidden_units), F32),
        ((ranks, width), F32), ((ranks, hidden_units), F32),
        ((ranks, hidden_units), F32), ((ranks, width), F32),
    ]
    anywhere = pl.BlockSpec(memory_space=pl.ANY)
    whole = pl.BlockSpec(memory_space=pltpu.VMEM)
    dma = pltpu.SemaphoreType.DMA
    outs = pl.pallas_call(
        functools.partial(kernel, (dp, nt, cap)),
        out_shape=[pltpu.VMEM(*form) for form in out_forms],
        in_specs=[anywhere] * 14,
        out_specs=[whole] * 8,
        scratch_shapes=[
            pltpu.VMEM((1, rows), jnp.int32),
            pltpu.VMEM((1, remaining_members.shape[0]), jnp.int32),
            pltpu.VMEM((1, allotment.shape[0]), jnp.int32),
            pltpu.VMEM((rows, width), BF16), pltpu.VMEM((rows, width), BF16),
            pltpu.VMEM((PARTS, rows, 2 * part), BF16), pltpu.VMEM((PARTS, rows, part), BF16),
            pltpu.VMEM((ranks, width), BF16), pltpu.VMEM((ranks, width), BF16),
            pltpu.VMEM((ranks, width), BF16),
            pltpu.VMEM((ranks, hidden_units), BF16), pltpu.VMEM((ranks, hidden_units), BF16),
            pltpu.VMEM((ranks, hidden_units), BF16),
            pltpu.VMEM((dp, cap, 128 + width), BF16), pltpu.VMEM((dp, cap, 128 + width), BF16),
            pltpu.VMEM((dp, cap, width), BF16), pltpu.VMEM((dp, cap, width), BF16),
            pltpu.VMEM((PARTS, dp, cap, 2 * part), BF16), pltpu.VMEM((PARTS, dp, cap, 2 * part), BF16),
            pltpu.VMEM((PARTS, dp, cap, part), BF16), pltpu.VMEM((PARTS, dp, cap, part), BF16),
            pltpu.VMEM((nt, 2 * RANK, slots), F32), pltpu.VMEM((nt, RANK, slots), F32),
            pltpu.VMEM((nt, RANK, slots), F32), pltpu.VMEM((nt, 2 * RANK, slots), F32),
            pltpu.VMEM((dp, cap, width), BF16), pltpu.VMEM((dp, cap, width), BF16),
            pltpu.VMEM((dp, cap, width), BF16), pltpu.VMEM((dp, cap, width), BF16),
            pltpu.VMEM((slots, hidden_units), F32), pltpu.VMEM((slots, hidden_units), F32),
            pltpu.VMEM((slots, hidden_units), BF16),
            pltpu.VMEM((slots, rows), BF16), pltpu.VMEM((rows, slots), BF16),
            pltpu.VMEM((slots, ranks), BF16), pltpu.VMEM((slots, ranks), BF16),
            pltpu.VMEM((slots, ranks), BF16),
            dma((11,)), dma((3, PARTS)),
            dma((4, dp)), dma((4, dp)), dma((2, PARTS, dp)), dma((2, PARTS, dp)),
            dma((4, nt)), dma((4, nt)),
        ],
        compiler_params=pltpu.CompilerParams(
            collective_id=0, has_side_effects=True, vmem_limit_bytes=38 * 2**20
        ),
        cost_estimate=pl.CostEstimate(flops=3 * 10**9, bytes_accessed=20 * 2**20, transcendentals=10**6),
    )(
        *[pltpu.with_memory_space_constraint(value, pltpu.HBM) for value in (
            sample_module_label.reshape(1, -1), remaining_members.reshape(1, -1), allotment.reshape(1, -1),
            block_source_vectors, fixed_switch_projection, fixed_expand_projection,
            result_adjoint_vectors, inner_activation_adjoint,
            switch_left_matrices.T, switch_right_matrices, expand_left_matrices.T,
            expand_right_matrices, contract_left_matrices.T, contract_right_matrices,
        )],
    )
    delta, gx, gag, gbg, gau, gbu, gad, gbd = pl.pallas_call(
        write_out,
        out_shape=[jax.ShapeDtypeStruct(*form) for form in out_forms],
        in_specs=[whole] * 8,
        out_specs=[anywhere] * 8,
        scratch_shapes=[dma((8,))],
        compiler_params=pltpu.CompilerParams(vmem_limit_bytes=2 * 2**20),
    )(*[pltpu.with_memory_space_constraint(value, pltpu.VMEM) for value in outs])
    return delta, gx, gag.T, gbg, gau.T, gbu, gad.T, gbd


def solution(mesh):
    rows = P(("groups", "dp"), "tensor")
    left = P(("groups", "tensor"), "dp")
    in_specs = (
        P("groups"), P("groups"), P(("groups", "dp")),
        rows, rows, rows, rows, rows,
        left, rows, left, rows, left, rows,
    )
    out_specs = (rows, rows, left, rows, left, rows, left, rows)
    return jax.shard_map(
        on_device, mesh=mesh, in_specs=in_specs, out_specs=out_specs, check_vma=False
    )
```
